32 devices in a mesh: groups: 2 (over x), exp: 8 (over z, y), seq: 2 (over core).
Axes of the slice: x: 2, y: 2, z: 4, core: 2. Of those that a mesh axis runs over, the one named last changes fastest.
Arguments:
- queries: bfloat16 [4096, 3584], P(('groups', 'exp'), 'seq'), parts along dimension 0, may hold values from -6 to 6
- key_rows: bfloat16 [4096, 3584], P(('groups', 'exp'), 'seq'), parts along dimension 0, may hold values from -6 to 6
- value_rows: bfloat16 [4096, 3584], P(('groups', 'exp'), 'seq'), parts along dimension 0, may hold values from -6 to 6
- residual: bfloat16 [4096, 3584], P(('groups', 'exp', 'seq')), parts along dimension 0, may hold values from -9 to 9
- norm_gain: float32 [3584], replicated, may hold values from 0.1 to 1.9
- router_weight: bfloat16 [3584, 8], replicated, may hold values from -0.09375 to 0.09375
- expert_ids: int32 [4096, 4], P(('groups', 'exp', 'seq')), parts along dimension 0, may hold values from 0 to 7, as said below
- gate_proj: bfloat16 [8, 3584, 768], P('exp', None, 'seq'), may hold values from -0.09375 to 0.09375
- up_proj: bfloat16 [8, 3584, 768], P('exp', None, 'seq'), may hold values from -0.09375 to 0.09375
- down_proj: bfloat16 [8, 768, 3584], P('exp', 'seq'), may hold values from -0.4375 to 0.4375
Outputs:
- mixed: bfloat16 [4096, 3584], P(('groups', 'exp', 'seq')), parts along dimension 0
The draws below stay inside these ranges and needn't reach their ends.
There are 2 independent parts, one for each index of `groups`. The reference program is written for one: setup_inputs(seed, part) draws one part's arguments, and reference() takes and returns one part's arrays. A program takes and returns all parts, laid end to end along the dimension named above; an argument that names none is the same for every part. Nothing has to cross between parts.
Inputs may be any that keep to these rules, and one draw needn't show every extreme that they name: `expert_ids`: each row names 4 different experts. Among the 512 entries of an aligned block of 128 tokens (the tokens of one device), no expert is named more than 96 times, and one expert is named exactly 96 times in every block.
All inputs are finite; a program needn't handle non-finite values.
Results may differ from the reference program's by a relative error of at most 0.014.
Values may be sent and summed in bfloat16 or wider, within the bound.
A program may use at most 128 MiB of HBM per device.

```python
import math
import jax
import jax.numpy as jnp
from jax import lax

D = 3584
HEADS = 28
HDIM = 128
FF = 768
TOP = 4
TOK_DEV = 128
SEQ_LEN = 256
TOKENS = 2048
EXPERTS = 8
CAP = 96


def draw_queries(key, part):
    key = jax.random.fold_in(key, 5)
    latents = TOKENS // SEQ_LEN
    draw_base = jax.random.truncated_normal(key, -6.0, 6.0, (latents, SEQ_LEN, D), jnp.float32)
    return draw_base.reshape(TOKENS, D).astype(jnp.bfloat16)


def draw_key_rows(key, part):
    key = jax.random.fold_in(key, 6)
    latents = TOKENS // SEQ_LEN
    draw_base = jax.random.truncated_normal(key, -6.0, 6.0, (latents, SEQ_LEN, D), jnp.float32)
    return draw_base.reshape(TOKENS, D).astype(jnp.bfloat16)


def draw_residual(key, part):
    key = jax.random.fold_in(key, 9)
    first_key = jax.random.fold_in(key, 0)
    third_key = jax.random.fold_in(key, 2)
    col_scale = jnp.exp(jax.random.uniform(first_key, (1, D), jnp.float32, math.log(0.3), math.log(3.0)))
    draw_base = jax.random.truncated_normal(third_key, -3.0, 3.0, (TOKENS, D), jnp.float32)
    return (draw_base * col_scale).astype(jnp.bfloat16)


def draw_expert_ids(key, part):
    key = jax.random.fold_in(key, 11)
    blocks = TOKENS // TOK_DEV
    unit_count = TOK_DEV // EXPERTS
    mean_count = TOP * unit_count
    half_spread = mean_count // 2
    hot_expert = jax.random.randint(jax.random.fold_in(key, 1), (), 0, EXPERTS)
    block_keys = jax.random.split(jax.random.fold_in(key, 2), blocks)

    def one_block(block_key):
        order_key, shift_key, row_key = jax.random.split(block_key, 3)
        order = jax.random.permutation(order_key, EXPERTS)
        spots = jnp.arange(EXPERTS)
        where_hot = jnp.sum(jnp.where(order == hot_expert, spots, 0))
        order = jnp.where(spots == 0, hot_expert, jnp.where(spots == where_hot, order[0], order))
        shifts = jax.random.randint(shift_key, (EXPERTS // 2,), -half_spread, half_spread + 1)
        shifts = shifts.at[0].set(half_spread)
        counts = jnp.stack([mean_count + shifts, mean_count - shifts], axis=1).reshape(EXPERTS)
        ends = jnp.cumsum(counts)
        flat_spots = jnp.arange(TOP * TOK_DEV)
        spot_of = jnp.sum((ends[None, :] <= flat_spots[:, None]).astype(jnp.int32), axis=1)
        names = order[spot_of]
        id_grid = names.reshape(TOP, TOK_DEV).T
        row_order = jax.random.permutation(row_key, TOK_DEV)
        return id_grid[row_order]
    return jax.vmap(one_block)(block_keys).reshape(TOKENS, TOP).astype(jnp.int32)


def block_levels(key, shape, pieces, low, largest):
    level = 1.0
    for axis_at, shards_of in pieces:
        steps = jax.random.uniform(jax.random.fold_in(jax.random.fold_in(key, 6), axis_at), (shards_of,), jnp.float32, low / len(pieces), largest / len(pieces))
        level = level * jnp.repeat(jnp.exp(steps), shape[axis_at] // shards_of).reshape((-1,) + (1,) * (len(shape) - 1 - axis_at))
    return level


def gaussian(key, shape, scale, bound, cuts=(), held_as=jnp.bfloat16):
    loudness = block_levels(key, shape, cuts, -0.22, 0.18) if cuts else 1.0
    entries = jax.random.normal(key, shape, jnp.float32) * scale * loudness
    return jnp.minimum(jnp.maximum(entries, -bound), bound).astype(held_as)


def setup_inputs(seed: int = 0, part: int = 0) -> dict:
    seeds = jax.random.split(jax.random.key(seed), 11)
    part_keys = jax.random.split(jax.random.fold_in(seeds[10], part), 11)
    queries = draw_queries(jax.random.fold_in(jax.random.fold_in(seeds[10], part), 71), part)
    key_rows = draw_key_rows(jax.random.fold_in(jax.random.fold_in(seeds[10], part), 71), part)
    value_rows = gaussian(part_keys[2], (TOKENS, D), 1.0, 6.0, ((0, 8), (1, 2)))
    residual = draw_residual(jax.random.fold_in(jax.random.fold_in(seeds[10], part), 71), part)
    norm_gain = jnp.clip(1.0 + 0.18 * jax.random.normal(seeds[4], (D,), jnp.float32), 0.1, 1.9)
    router_weight = gaussian(seeds[5], (D, EXPERTS), D ** -0.5, 0.09375)
    expert_ids = draw_expert_ids(jax.random.fold_in(jax.random.fold_in(seeds[10], part), 71), part)
    gate_proj = gaussian(seeds[7], (EXPERTS, D, FF), D ** -0.5, 0.09375, ((0, 8), (2, 2)))
    up_proj = gaussian(seeds[8], (EXPERTS, D, FF), D ** -0.5, 0.09375, ((0, 8), (2, 2)))
    down_proj = gaussian(seeds[9], (EXPERTS, FF, D), (FF // 4) ** -0.5, 0.4375, ((0, 8), (1, 2)))
    return dict(queries=queries, key_rows=key_rows, value_rows=value_rows, residual=residual, norm_gain=norm_gain, router_weight=router_weight, expert_ids=expert_ids, gate_proj=gate_proj, up_proj=up_proj, down_proj=down_proj)


epsilon = 1e-06

def attend_latent(latent_blocks):
    query_part, key_part, value_part = latent_blocks
    shaped_q = query_part.reshape(SEQ_LEN, HEADS, HDIM).astype(jnp.float32)
    shaped_k = key_part.reshape(SEQ_LEN, HEADS, HDIM).astype(jnp.float32)
    shaped_v = value_part.reshape(SEQ_LEN, HEADS, HDIM).astype(jnp.float32)
    scores = jnp.einsum('qhd,khd->hqk', shaped_q, shaped_k) * HDIM ** (-0.5)
    row_top = lax.optimization_barrier(jnp.max(scores, axis=-1, keepdims=True))
    exp_scores = jnp.exp(scores - row_top)
    row_total = lax.optimization_barrier(jnp.sum(exp_scores, axis=-1))
    weights = lax.optimization_barrier(exp_scores.astype(jnp.bfloat16)).astype(jnp.float32)
    mixed_heads = jnp.einsum('hqk,khd->qhd', weights, shaped_v) / jnp.transpose(row_total)[:, :, None]
    return mixed_heads.astype(jnp.bfloat16).reshape(SEQ_LEN, HEADS * HDIM)

def expert_half(row_block, gate_cols, up_cols, down_rows):
    gate_out = jnp.dot(row_block, gate_cols, preferred_element_type=jnp.float32)
    up_out = jnp.dot(row_block, up_cols, preferred_element_type=jnp.float32)
    middle = (jax.nn.silu(gate_out) * up_out).astype(jnp.bfloat16)
    return jnp.dot(middle, down_rows, preferred_element_type=jnp.float32).astype(jnp.bfloat16)

def reference(queries, key_rows, value_rows, residual, norm_gain, router_weight, expert_ids, gate_proj, up_proj, down_proj):
    latents = TOKENS // SEQ_LEN
    attended = lax.map(attend_latent, (queries.reshape(latents, SEQ_LEN, D), key_rows.reshape(latents, SEQ_LEN, D), value_rows.reshape(latents, SEQ_LEN, D))).reshape(TOKENS, D)
    hidden = (residual.astype(jnp.float32) + attended.astype(jnp.float32)).astype(jnp.bfloat16)
    hidden_f = hidden.astype(jnp.float32)
    mean_sq = lax.optimization_barrier(jnp.mean(hidden_f * hidden_f, axis=-1, keepdims=True))
    normed = (hidden_f * lax.rsqrt(mean_sq + epsilon) * norm_gain.astype(jnp.float32)).astype(jnp.bfloat16)
    logits = jnp.dot(normed, router_weight, preferred_element_type=jnp.float32)
    picked = jnp.take_along_axis(logits, expert_ids, axis=1)
    sigmoids = jax.nn.sigmoid(picked)
    gate_values = sigmoids / lax.optimization_barrier(jnp.sum(sigmoids, axis=1, keepdims=True))
    blocks = TOKENS // TOK_DEV
    flat_ids = expert_ids.reshape(blocks, TOK_DEV * TOP)
    onehot = (flat_ids[:, :, None] == jnp.arange(EXPERTS, dtype=jnp.int32)[None, None, :]).astype(jnp.int32)
    earlier = jnp.cumsum(onehot, axis=1) - onehot
    slot_index = lax.optimization_barrier(jnp.sum(earlier * onehot, axis=2)).reshape(TOKENS, TOP)
    token_index = jnp.arange(TOKENS, dtype=jnp.int32)
    column = ((token_index // TOK_DEV)[:, None] * CAP + slot_index).astype(jnp.int32)
    token_grid = jnp.broadcast_to(token_index[:, None], (TOKENS, TOP))
    slot_table = jnp.full((EXPERTS, blocks * CAP), TOKENS, dtype=jnp.int32).at[expert_ids, column].set(token_grid)
    gate_table = jnp.zeros((EXPERTS, blocks * CAP), jnp.float32).at[expert_ids, column].set(gate_values)
    padded = jnp.concatenate([normed, jnp.zeros((1, D), jnp.bfloat16)], axis=0)
    half_width = FF // 2

    def one_expert(accumulated, expert):
        row_block = padded[slot_table[expert]]
        gate_all = gate_proj[expert]
        up_all = up_proj[expert]
        down_all = down_proj[expert]
        half_parts = []
        for half_index in range(2):
            start_col = half_index * half_width
            half_piece = expert_half(row_block, gate_all[:, start_col:start_col + half_width], up_all[:, start_col:start_col + half_width], down_all[start_col:start_col + half_width, :])
            half_parts.append(lax.optimization_barrier(half_piece).astype(jnp.float32))
        merged = (half_parts[0] + half_parts[1]).astype(jnp.bfloat16)
        contrib = gate_table[expert][:, None] * merged.astype(jnp.float32)
        accumulated = accumulated.at[slot_table[expert]].add(contrib, mode='drop')
        return (accumulated, None)
    accumulated, unused = lax.scan(one_expert, jnp.zeros((TOKENS, D), jnp.float32), jnp.arange(EXPERTS, dtype=jnp.int32))
    return (hidden_f + accumulated).astype(jnp.bfloat16)
```

```python
import jax
import jax.numpy as jnp
from jax import lax
from jax.experimental import pallas as pl
from jax.experimental.pallas import tpu as pltpu
from jax.sharding import PartitionSpec as P

HDIM = 128
TOP = 4


epsilon = 1e-06


def head_attention(query_block, key_block, value_block):
    scores = jnp.einsum(
        "qhd,khd->hqk", query_block, key_block, preferred_element_type=jnp.float32
    ) * HDIM ** (-0.5)
    row_top = jnp.max(scores, axis=-1, keepdims=True)
    exp_scores = jnp.exp(scores - row_top)
    row_total = jnp.sum(exp_scores, axis=-1)
    mixed_heads = (
        jnp.einsum(
            "hqk,khd->qhd",
            exp_scores.astype(jnp.bfloat16),
            value_block,
            preferred_element_type=jnp.float32,
        )
        / jnp.transpose(row_total)[:, :, None]
    )
    return mixed_heads.astype(jnp.bfloat16)


def expert_partial(row_block, gate_cols, up_cols, down_rows):
    gate_out = jnp.dot(row_block, gate_cols, preferred_element_type=jnp.float32)
    up_out = jnp.dot(row_block, up_cols, preferred_element_type=jnp.float32)
    middle = (jax.nn.silu(gate_out) * up_out).astype(jnp.bfloat16)
    return jnp.dot(middle, down_rows, preferred_element_type=jnp.float32)


def by_slots(
    queries,
    key_rows,
    value_rows,
    residual,
    norm_gain,
    router_weight,
    expert_ids,
    gate_proj,
    up_proj,
    down_proj,
):
    local_tokens = residual.shape[0]
    model_width = residual.shape[1]
    latent_rows = queries.shape[0]
    head_cols = queries.shape[1]
    heads_here = head_cols // HDIM
    local_heads = head_attention(
        queries.reshape(latent_rows, heads_here, HDIM),
        key_rows.reshape(latent_rows, heads_here, HDIM),
        value_rows.reshape(latent_rows, heads_here, HDIM),
    )
    attended = lax.all_to_all(
        local_heads.reshape(latent_rows, head_cols), "seq", split_axis=0, concat_axis=1, tiled=True
    )
    hidden = (residual.astype(jnp.float32) + attended.astype(jnp.float32)).astype(jnp.bfloat16)
    hidden_f = hidden.astype(jnp.float32)
    mean_sq = jnp.mean(hidden_f * hidden_f, axis=-1, keepdims=True)
    normed = (hidden_f * lax.rsqrt(mean_sq + epsilon) * norm_gain).astype(jnp.bfloat16)
    logits = jnp.dot(normed, router_weight, preferred_element_type=jnp.float32)
    experts = router_weight.shape[1]
    capacity = 3 * local_tokens * TOP // (2 * experts)
    catalog = jnp.arange(experts, dtype=jnp.int32)
    flat_ids = expert_ids.reshape(local_tokens * TOP)
    onehot = (flat_ids[:, None] == catalog[None, :]).astype(jnp.int32)
    picked = jnp.sum(
        onehot.reshape(local_tokens, TOP, experts).astype(jnp.float32) * logits[:, None, :], axis=2
    )
    sigmoids = jax.nn.sigmoid(picked)
    gate_values = sigmoids / jnp.sum(sigmoids, axis=1, keepdims=True)
    earlier = jnp.cumsum(onehot, axis=0) - onehot
    slot_index = jnp.sum(earlier * onehot, axis=1)
    place = flat_ids * capacity + slot_index
    source_rows = jnp.repeat(normed, TOP, axis=0)
    outgoing = (
        jnp.zeros((experts * capacity, model_width), jnp.bfloat16)
        .at[place]
        .set(source_rows)
        .reshape(experts, capacity, model_width)
    )
    both_halves = lax.all_gather(
        lax.all_to_all(outgoing, "exp", split_axis=0, concat_axis=0, tiled=True),
        "seq",
        axis=0,
        tiled=True,
    )
    partial_value = expert_partial(
        both_halves.reshape(-1, model_width), gate_proj[0], up_proj[0], down_proj[0]
    ).reshape(both_halves.shape)
    summed = lax.psum_scatter(
        partial_value.astype(jnp.bfloat16), "seq", scatter_dimension=0, tiled=True
    )
    answers = lax.all_to_all(summed, "exp", split_axis=0, concat_axis=0, tiled=True)
    returned_rows = answers.reshape(experts * capacity, model_width)
    gathered = returned_rows[place].reshape(local_tokens, TOP, model_width)
    moe_sum = hidden_f
    for which_slot in range(TOP):
        moe_sum = moe_sum + gate_values[:, which_slot : which_slot + 1] * gathered[
            :, which_slot
        ].astype(jnp.float32)
    return moe_sum.astype(jnp.bfloat16)


def attention_kernel(q_ref, k_ref, v_ref, o_ref):
    for at in range(q_ref.shape[1] // HDIM):
        cols = slice(at * HDIM, (at + 1) * HDIM)
        scores = lax.dot_general(
            q_ref[:, cols],
            k_ref[:, cols],
            (((1,), (1,)), ((), ())),
            preferred_element_type=jnp.float32,
        ) * HDIM ** (-0.5)
        exp_scores = jnp.exp(scores - jnp.max(scores, axis=-1, keepdims=True))
        row_total = jnp.sum(exp_scores, axis=-1, keepdims=True)
        mixed_head = jnp.dot(
            exp_scores.astype(jnp.bfloat16), v_ref[:, cols], preferred_element_type=jnp.float32
        )
        o_ref[:, cols] = (mixed_head / row_total).astype(o_ref.dtype)


def attention(queries, key_rows, value_rows):
    rows, cols = queries.shape
    width = 2 * HDIM
    spec = pl.BlockSpec((rows, width), lambda h: (0, h))
    return pl.pallas_call(
        attention_kernel,
        grid=(cols // width,),
        in_specs=[spec] * 3,
        out_specs=spec,
        out_shape=jax.ShapeDtypeStruct((rows, cols), jnp.bfloat16),
        cost_estimate=pl.CostEstimate(
            flops=4 * rows * rows * cols,
            bytes_accessed=8 * rows * cols,
            transcendentals=rows * rows * cols // HDIM,
        ),
    )(queries, key_rows, value_rows)


def hidden_and_normed(queries, key_rows, value_rows, residual, norm_gain):
    attended = lax.all_to_all(
        attention(queries, key_rows, value_rows), "seq", split_axis=0, concat_axis=1, tiled=True
    )
    hidden = (residual.astype(jnp.float32) + attended.astype(jnp.float32)).astype(jnp.bfloat16)
    hidden_f = hidden.astype(jnp.float32)
    mean_sq = jnp.mean(hidden_f * hidden_f, axis=-1, keepdims=True)
    normed = (hidden_f * lax.rsqrt(mean_sq + epsilon) * norm_gain).astype(jnp.bfloat16)
    return hidden, normed


def own_gates(rows, ids, router_weight):
    experts = router_weight.shape[1]
    logits = jnp.dot(rows, router_weight, preferred_element_type=jnp.float32)
    catalog = jnp.arange(experts, dtype=jnp.int32)
    chosen = jnp.any(ids[:, :, None] == catalog[None, None, :], axis=1)
    sigmoids = jnp.where(chosen, jax.nn.sigmoid(logits), 0.0)
    gates = sigmoids / jnp.sum(sigmoids, axis=1, keepdims=True)
    mine = catalog == lax.axis_index("exp")
    return jnp.sum(jnp.where(mine[None, :], gates, 0.0), axis=1, keepdims=True)


def by_rows(
    queries,
    key_rows,
    value_rows,
    residual,
    norm_gain,
    router_weight,
    expert_ids,
    gate_proj,
    up_proj,
    down_proj,
):
    ids = lax.all_gather(expert_ids, "exp", axis=0, tiled=True)
    gate_all = lax.all_gather(gate_proj[0], "seq", axis=1, tiled=True)
    up_all = lax.all_gather(up_proj[0], "seq", axis=1, tiled=True)
    down_all = lax.all_gather(down_proj[0], "seq", axis=0, tiled=True)
    hidden, normed = hidden_and_normed(queries, key_rows, value_rows, residual, norm_gain)
    rows = lax.all_gather(normed, "exp", axis=0, tiled=True)
    gates = own_gates(rows, ids, router_weight)
    weighted = gates * expert_partial(rows, gate_all, up_all, down_all)
    summed = lax.psum_scatter(
        weighted.astype(jnp.bfloat16), "exp", scatter_dimension=0, tiled=True
    )
    return (hidden.astype(jnp.float32) + summed.astype(jnp.float32)).astype(jnp.bfloat16)


def solution(mesh):
    return jax.shard_map(
        by_rows if mesh.shape["exp"] <= 8 else by_slots,
        mesh=mesh,
        in_specs=(
            P(("groups", "exp"), "seq"),
            P(("groups", "exp"), "seq"),
            P(("groups", "exp"), "seq"),
            P(("groups", "exp", "seq"), None),
            P(),
            P(),
            P(("groups", "exp", "seq"), None),
            P("exp", None, "seq"),
            P("exp", None, "seq"),
            P("exp", "seq", None),
        ),
        out_specs=P(("groups", "exp", "seq"), None),
        check_vma=False,
    )
```

```python
import functools

import jax
import jax.numpy as jnp
from jax import lax
from jax.experimental import pallas as pl
from jax.experimental.pallas import tpu as pltpu
from jax.sharding import PartitionSpec as P

HDIM = 128
TOP = 4


epsilon = 1e-06


def head_attention(query_block, key_block, value_block):
    scores = jnp.einsum(
        "qhd,khd->hqk", query_block, key_block, preferred_element_type=jnp.float32
    ) * HDIM ** (-0.5)
    row_top = jnp.max(scores, axis=-1, keepdims=True)
    exp_scores = jnp.exp(scores - row_top)
    row_total = jnp.sum(exp_scores, axis=-1)
    mixed_heads = (
        jnp.einsum(
            "hqk,khd->qhd",
            exp_scores.astype(jnp.bfloat16),
            value_block,
            preferred_element_type=jnp.float32,
        )
        / jnp.transpose(row_total)[:, :, None]
    )
    return mixed_heads.astype(jnp.bfloat16)


def expert_partial(row_block, gate_cols, up_cols, down_rows):
    gate_out = jnp.dot(row_block, gate_cols, preferred_element_type=jnp.float32)
    up_out = jnp.dot(row_block, up_cols, preferred_element_type=jnp.float32)
    middle = (jax.nn.silu(gate_out) * up_out).astype(jnp.bfloat16)
    return jnp.dot(middle, down_rows, preferred_element_type=jnp.float32)


def by_slots(
    queries,
    key_rows,
    value_rows,
    residual,
    norm_gain,
    router_weight,
    expert_ids,
    gate_proj,
    up_proj,
    down_proj,
):
    local_tokens = residual.shape[0]
    model_width = residual.shape[1]
    latent_rows = queries.shape[0]
    head_cols = queries.shape[1]
    heads_here = head_cols // HDIM
    local_heads = head_attention(
        queries.reshape(latent_rows, heads_here, HDIM),
        key_rows.reshape(latent_rows, heads_here, HDIM),
        value_rows.reshape(latent_rows, heads_here, HDIM),
    )
    attended = lax.all_to_all(
        local_heads.reshape(latent_rows, head_cols), "seq", split_axis=0, concat_axis=1, tiled=True
    )
    hidden = (residual.astype(jnp.float32) + attended.astype(jnp.float32)).astype(jnp.bfloat16)
    hidden_f = hidden.astype(jnp.float32)
    mean_sq = jnp.mean(hidden_f * hidden_f, axis=-1, keepdims=True)
    normed = (hidden_f * lax.rsqrt(mean_sq + epsilon) * norm_gain).astype(jnp.bfloat16)
    logits = jnp.dot(normed, router_weight, preferred_element_type=jnp.float32)
    experts = router_weight.shape[1]
    capacity = 3 * local_tokens * TOP // (2 * experts)
    catalog = jnp.arange(experts, dtype=jnp.int32)
    flat_ids = expert_ids.reshape(local_tokens * TOP)
    onehot = (flat_ids[:, None] == catalog[None, :]).astype(jnp.int32)
    picked = jnp.sum(
        onehot.reshape(local_tokens, TOP, experts).astype(jnp.float32) * logits[:, None, :], axis=2
    )
    sigmoids = jax.nn.sigmoid(picked)
    gate_values = sigmoids / jnp.sum(sigmoids, axis=1, keepdims=True)
    earlier = jnp.cumsum(onehot, axis=0) - onehot
    slot_index = jnp.sum(earlier * onehot, axis=1)
    place = flat_ids * capacity + slot_index
    source_rows = jnp.repeat(normed, TOP, axis=0)
    outgoing = (
        jnp.zeros((experts * capacity, model_width), jnp.bfloat16)
        .at[place]
        .set(source_rows)
        .reshape(experts, capacity, model_width)
    )
    both_halves = lax.all_gather(
        lax.all_to_all(outgoing, "exp", split_axis=0, concat_axis=0, tiled=True),
        "seq",
        axis=0,
        tiled=True,
    )
    partial_value = expert_partial(
        both_halves.reshape(-1, model_width), gate_proj[0], up_proj[0], down_proj[0]
    ).reshape(both_halves.shape)
    summed = lax.psum_scatter(
        partial_value.astype(jnp.bfloat16), "seq", scatter_dimension=0, tiled=True
    )
    answers = lax.all_to_all(summed, "exp", split_axis=0, concat_axis=0, tiled=True)
    returned_rows = answers.reshape(experts * capacity, model_width)
    gathered = returned_rows[place].reshape(local_tokens, TOP, model_width)
    moe_sum = hidden_f
    for which_slot in range(TOP):
        moe_sum = moe_sum + gate_values[:, which_slot : which_slot + 1] * gathered[
            :, which_slot
        ].astype(jnp.float32)
    return moe_sum.astype(jnp.bfloat16)


def attention_kernel(q_ref, k_ref, v_ref, o_ref):
    for at in range(q_ref.shape[1] // HDIM):
        cols = slice(at * HDIM, (at + 1) * HDIM)
        scores = lax.dot_general(
            q_ref[:, cols],
            k_ref[:, cols],
            (((1,), (1,)), ((), ())),
            preferred_element_type=jnp.float32,
        ) * HDIM ** (-0.5)
        exp_scores = jnp.exp(scores - jnp.max(scores, axis=-1, keepdims=True))
        row_total = jnp.sum(exp_scores, axis=-1, keepdims=True)
        mixed_head = jnp.dot(
            exp_scores.astype(jnp.bfloat16), v_ref[:, cols], preferred_element_type=jnp.float32
        )
        o_ref[:, cols] = (mixed_head / row_total).astype(o_ref.dtype)


def attention(queries, key_rows, value_rows):
    rows, cols = queries.shape
    width = 2 * HDIM
    spec = pl.BlockSpec((rows, width), lambda h: (0, h))
    return pl.pallas_call(
        attention_kernel,
        grid=(cols // width,),
        in_specs=[spec] * 3,
        out_specs=spec,
        out_shape=jax.ShapeDtypeStruct((rows, cols), jnp.bfloat16),
        cost_estimate=pl.CostEstimate(
            flops=4 * rows * rows * cols,
            bytes_accessed=8 * rows * cols,
            transcendentals=rows * rows * cols // HDIM,
        ),
    )(queries, key_rows, value_rows)


def hidden_and_normed(queries, key_rows, value_rows, residual, norm_gain):
    attended = lax.all_to_all(
        attention(queries, key_rows, value_rows), "seq", split_axis=0, concat_axis=1, tiled=True
    )
    hidden = (residual.astype(jnp.float32) + attended.astype(jnp.float32)).astype(jnp.bfloat16)
    hidden_f = hidden.astype(jnp.float32)
    mean_sq = jnp.mean(hidden_f * hidden_f, axis=-1, keepdims=True)
    normed = (hidden_f * lax.rsqrt(mean_sq + epsilon) * norm_gain).astype(jnp.bfloat16)
    return hidden, normed


SHARED = 16
MESH = pl.DeviceIdType.MESH


def dense_gates(normed, ids, router_weight):
    experts = router_weight.shape[1]
    logits = jnp.dot(normed, router_weight, preferred_element_type=jnp.float32)
    catalog = jnp.arange(experts, dtype=jnp.int32)
    chosen = jnp.any(ids[:, :, None] == catalog[None, None, :], axis=1)
    sigmoids = jnp.where(chosen, jax.nn.sigmoid(logits), 0.0)
    return sigmoids / jnp.sum(sigmoids, axis=1, keepdims=True)


def expert_kernel(
    owners,
    normed_ref,
    gates_ref,
    gate_ref,
    up_ref,
    down_ref,
    out_ref,
    rows,
    sums,
    from_side,
    from_below,
    from_above,
    gate_all,
    up_all,
    down_all,
    middle,
    gates,
    local_sem,
    weight_send,
    weight_recv,
    gates_send,
    gates_recv,
    shared_sems,
    side_send,
    side_recv,
    up_send,
    down_send,
    line_recv,
    back_side_send,
    back_side_recv,
    back_up_send,
    back_up_recv,
    back_down_send,
    back_down_recv,
    last_sems,
):
    length = owners // 2
    tokens, width = normed_ref.shape
    half = gate_ref.shape[1]
    apart = tokens - SHARED
    me = lax.axis_index("exp")
    core = lax.axis_index("seq")
    z = me // 2
    y = me % 2
    side = {"exp": me + 1 - 2 * y}
    other_core = {"seq": 1 - core}
    above = {"exp": me + 2}
    below = {"exp": me - 2}
    has_above = z + 1 < length
    has_below = z > 0

    def start_of(count):
        return pl.multiple_of(count, 16)

    line_rows = pl.ds(start_of(y * apart), tokens + SHARED)
    my_apart = pl.ds(start_of(y * (tokens + SHARED)), apart)
    side_apart = pl.ds(start_of((1 - y) * (tokens + SHARED)), apart)
    my_shared = pl.ds(start_of(apart + y * SHARED), SHARED)
    side_shared = pl.ds(start_of(apart + (1 - y) * SHARED), SHARED)
    own_rows = pl.ds(start_of(y * tokens), tokens)

    def remote(src, dst, send, recv, device):
        return pltpu.make_async_remote_copy(
            src_ref=src, dst_ref=dst, send_sem=send, recv_sem=recv, device_id=device, device_id_type=MESH
        )

    def own_weights(at):
        src = (gate_ref, up_ref, down_ref)[at]
        dst = (
            gate_all.at[:, pl.ds(0, half)],
            up_all.at[:, pl.ds(0, half)],
            down_all.at[pl.ds(0, half)],
        )[at]
        return pltpu.make_async_copy(src, dst, local_sem.at[at])

    def other_weights(at):
        src = (gate_ref, up_ref, down_ref)[at]
        dst = (
            gate_all.at[:, pl.ds(half, half)],
            up_all.at[:, pl.ds(half, half)],
            down_all.at[pl.ds(half, half)],
        )[at]
        return remote(src, dst, weight_send.at[at], weight_recv.at[at], other_core)

    def gates_copy(step):
        to = lax.rem(me + step, owners)
        return remote(
            gates_ref, gates.at[me], gates_send.at[step], gates_recv.at[step], {"exp": to}
        )

    def shared_copy():
        return remote(
            rows.at[z, my_shared], rows.at[z, my_shared], shared_sems.at[0], shared_sems.at[1], side
        )

    def side_copy(at):
        return remote(
            rows.at[at, my_apart], rows.at[at, my_apart], side_send.at[at], side_recv.at[at], side
        )

    def up_copy(at):
        return remote(
            rows.at[at, line_rows], rows.at[at, line_rows], up_send.at[at], line_recv.at[at], above
        )

    def down_copy(at):
        return remote(
            rows.at[at, line_rows], rows.at[at, line_rows], down_send.at[at], line_recv.at[at], below
        )

    def back_side_copy(at):
        return remote(
            sums.at[at, side_apart],
            from_side.at[at],
            back_side_send.at[at],
            back_side_recv.at[at],
            side,
        )

    def back_up_copy(at):
        return remote(
            sums.at[at, line_rows],
            from_below.at[at],
            back_up_send.at[at],
            back_up_recv.at[at],
            above,
        )

    def back_down_copy(at):
        return remote(
            sums.at[at, line_rows],
            from_above.at[at],
            back_down_send.at[at],
            back_down_recv.at[at],
            below,
        )

    def last_copy():
        return remote(
            sums.at[z, side_shared],
            from_side.at[length, pl.ds(0, SHARED)],
            last_sems.at[0],
            last_sems.at[1],
            side,
        )

    barrier = pltpu.get_barrier_semaphore()
    for step in range(1, owners):
        pl.semaphore_signal(
            barrier, inc=1, device_id={"exp": lax.rem(me + step, owners)}, device_id_type=MESH
        )
    pl.semaphore_signal(barrier, inc=1, device_id=other_core, device_id_type=MESH)
    own_copy = pltpu.make_async_copy(normed_ref, rows.at[z, own_rows], local_sem.at[3])
    own_copy.start()
    own_gates = pltpu.make_async_copy(gates_ref, gates.at[me], local_sem.at[4])
    own_gates.start()
    own_copy.wait()
    pl.semaphore_wait(barrier, owners)

    shared_copy().start()
    side_copy(z).start()
    for step in range(1, owners):
        gates_copy(step).start()
    for at in range(3):
        other_weights(at).start()
    for at in range(3):
        own_weights(at).start()
    shared_copy().wait_recv()

    @pl.when(has_above)
    def _():
        up_copy(z).start()

    @pl.when(has_below)
    def _():
        down_copy(z).start()

    own_gates.wait()
    for step in range(1, owners):
        gates_copy(step).wait_recv()
    for at in range(3):
        own_weights(at).wait()
        other_weights(at).wait_recv()

    def expert_sums(at):
        grid_row = lax.broadcasted_iota(jnp.int32, (tokens, tokens), 0)
        grid_col = lax.broadcasted_iota(jnp.int32, (tokens, tokens), 1)

        def gate_column(which):
            table = gates[2 * at + which]
            mine = lax.broadcasted_iota(jnp.int32, table.shape, 0) == me
            line = jnp.sum(jnp.where(mine, table, 0.0), axis=0, keepdims=True)
            return jnp.sum(jnp.where(grid_row == grid_col, line, 0.0), axis=1, keepdims=True)

        gate_col = jnp.concatenate([gate_column(0), gate_column(1)], axis=0)

        def middle_tile(tile, carry):
            cols = pl.ds(pl.multiple_of(tile * 256, 256), 256)
            gate_out = jnp.dot(rows[at], gate_all[:, cols], preferred_element_type=jnp.float32)
            up_out = jnp.dot(rows[at], up_all[:, cols], preferred_element_type=jnp.float32)
            middle[:, cols] = (gate_out / (1.0 + jnp.exp(-gate_out)) * up_out).astype(jnp.bfloat16)
            return carry

        lax.fori_loop(0, 2 * half // 256, middle_tile, 0)

        def out_tile(tile, carry):
            cols = pl.ds(pl.multiple_of(tile * 512, 512), 512)
            part = jnp.dot(middle[...], down_all[:, cols], preferred_element_type=jnp.float32)
            sums[at, :, cols] = (part * gate_col).astype(jnp.bfloat16)
            return carry

        lax.fori_loop(0, width // 512, out_tile, 0)

    def place(step):
        away = (step + 1) // 2
        return jnp.where(step % 2 == 1, z - away, z + away)

    def inside(at):
        return jnp.logical_and(at >= 0, at < length)

    def gather_step(step):
        at = place(step)

        @pl.when(inside(at))
        def _():
            up_copy(at).wait_recv()

            @pl.when(jnp.logical_and(at < z, has_above))
            def _():
                up_copy(at).start()

            @pl.when(jnp.logical_and(at > z, has_below))
            def _():
                down_copy(at).start()

            side_copy(at).start()

    def compute_step(step):
        at = place(step)

        @pl.when(inside(at))
        def _():
            side_copy(at).wait_recv()
            expert_sums(at)
            back_side_copy(at).start()

    steps = 2 * length - 1

    def gather_and_compute(step, carry):
        @pl.when(jnp.logical_and(step >= 1, step < steps))
        def _():
            gather_step(step)

        @pl.when(step >= 2)
        def _():
            compute_step(step - 2)

        return carry

    lax.fori_loop(0, steps + 2, gather_and_compute, 0)

    def add_rows(at, first, source, first_source, count):
        def add_some(piece, carry):
            into = pl.ds(start_of(first + piece * 16), 16)
            what = pl.ds(start_of(first_source + piece * 16), 16)
            sums[at, into] = (
                sums[at, into].astype(jnp.float32) + source[at, what].astype(jnp.float32)
            ).astype(jnp.bfloat16)
            return carry

        lax.fori_loop(0, count // 16, add_some, 0)

    def add_side(at):
        back_side_copy(at).wait_recv()
        add_rows(at, y * (tokens + SHARED), from_side, 0, apart)

    def add_below(at):
        back_up_copy(at).wait_recv()
        add_rows(at, y * apart, from_below, 0, tokens + SHARED)

    def add_above(at):
        back_down_copy(at).wait_recv()
        add_rows(at, y * apart, from_above, 0, tokens + SHARED)

    def return_step(step, carry):
        high = length - 1 - step

        @pl.when(high > z)
        def _():
            add_side(high)

            @pl.when(has_below)
            def _():
                add_below(high)

            back_up_copy(high).start()

        @pl.when(step < z)
        def _():
            add_side(step)

            @pl.when(has_above)
            def _():
                add_above(step)

            back_down_copy(step).start()

        return carry

    lax.fori_loop(0, length - 1, return_step, 0)
    add_side(z)

    @pl.when(has_below)
    def _():
        add_below(z)

    @pl.when(has_above)
    def _():
        add_above(z)

    last_copy().start()
    out_ref[...] = sums[z, own_rows]
    last_copy().wait_recv()
    out_shared = pl.ds(start_of((1 - y) * apart), SHARED)
    out_ref[out_shared] = (
        out_ref[out_shared].astype(jnp.float32)
        + from_side[length, pl.ds(0, SHARED)].astype(jnp.float32)
    ).astype(jnp.bfloat16)

    last_copy().wait_send()
    shared_copy().wait_send()
    for step in range(1, owners):
        gates_copy(step).wait_send()
    for at in range(3):
        other_weights(at).wait_send()

    def drain(at, carry):
        side_copy(at).wait_send()
        back_side_copy(at).wait_send()

        @pl.when(jnp.logical_and(at <= z, has_above))
        def _():
            up_copy(at).wait_send()

        @pl.when(jnp.logical_and(at >= z, has_below))
        def _():
            down_copy(at).wait_send()

        @pl.when(at > z)
        def _():
            back_up_copy(at).wait_send()

        @pl.when(at < z)
        def _():
            back_down_copy(at).wait_send()

        return carry

    lax.fori_loop(0, length, drain, 0)


def routed_experts(normed, gates, gate_half, up_half, down_half):
    tokens, width = normed.shape
    owners = gates.shape[0]
    length = owners // 2
    half = gate_half.shape[1]
    anywhere = pl.BlockSpec(memory_space=pl.ANY)
    dma = pltpu.SemaphoreType.DMA
    return pl.pallas_call(
        functools.partial(expert_kernel, owners),
        in_specs=[anywhere] * 5,
        out_specs=pl.BlockSpec(memory_space=pltpu.VMEM),
        out_shape=jax.ShapeDtypeStruct((tokens, width), jnp.bfloat16),
        scratch_shapes=[
            pltpu.VMEM((length, 2 * tokens, width), jnp.bfloat16),
            pltpu.VMEM((length, 2 * tokens, width), jnp.bfloat16),
            pltpu.VMEM((length + 1, tokens - SHARED, width), jnp.bfloat16),
            pltpu.VMEM((length, tokens + SHARED, width), jnp.bfloat16),
            pltpu.VMEM((length, tokens + SHARED, width), jnp.bfloat16),
            pltpu.VMEM((width, 2 * half), jnp.bfloat16),
            pltpu.VMEM((width, 2 * half), jnp.bfloat16),
            pltpu.VMEM((2 * half, width), jnp.bfloat16),
            pltpu.VMEM((2 * tokens, 2 * half), jnp.bfloat16),
            pltpu.VMEM((owners, owners, tokens), jnp.float32),
            dma((5,)),
            dma((3,)),
            dma((3,)),
            dma((owners,)),
            dma((owners,)),
            dma((2,)),
        ]
        + [dma((length,))] * 11
        + [dma((2,))],
        compiler_params=pltpu.CompilerParams(
            collective_id=0, has_side_effects=True, vmem_limit_bytes=58 * 1024 * 1024
        ),
        cost_estimate=pl.CostEstimate(
            flops=12 * owners * tokens * width * half,
            bytes_accessed=12 * width * half,
            transcendentals=2 * owners * tokens * half,
        ),
    )(normed, gates, gate_half, up_half, down_half)


def by_rows(
    queries,
    key_rows,
    value_rows,
    residual,
    norm_gain,
    router_weight,
    expert_ids,
    gate_proj,
    up_proj,
    down_proj,
):
    hidden, normed = hidden_and_normed(queries, key_rows, value_rows, residual, norm_gain)
    gates = jnp.transpose(dense_gates(normed, expert_ids, router_weight))
    summed = routed_experts(normed, gates, gate_proj[0], up_proj[0], down_proj[0])
    return (hidden.astype(jnp.float32) + summed.astype(jnp.float32)).astype(jnp.bfloat16)


def solution(mesh):
    return jax.shard_map(
        by_rows if mesh.shape["exp"] == 8 else by_slots,
        mesh=mesh,
        in_specs=(
            P(("groups", "exp"), "seq"),
            P(("groups", "exp"), "seq"),
            P(("groups", "exp"), "seq"),
            P(("groups", "exp", "seq"), None),
            P(),
            P(),
            P(("groups", "exp", "seq"), None),
            P("exp", None, "seq"),
            P("exp", None, "seq"),
            P("exp", "seq", None),
        ),
        out_specs=P(("groups", "exp", "seq"), None),
        check_vma=False,
    )
```

```python
import functools

import jax
import jax.numpy as jnp
from jax import lax
from jax.experimental import pallas as pl
from jax.experimental.pallas import tpu as pltpu
from jax.sharding import PartitionSpec as P

HDIM = 128
TOP = 4


epsilon = 1e-06


def head_attention(query_block, key_block, value_block):
    scores = jnp.einsum(
        "qhd,khd->hqk", query_block, key_block, preferred_element_type=jnp.float32
    ) * HDIM ** (-0.5)
    row_top = jnp.max(scores, axis=-1, keepdims=True)
    exp_scores = jnp.exp(scores - row_top)
    row_total = jnp.sum(exp_scores, axis=-1)
    mixed_heads = (
        jnp.einsum(
            "hqk,khd->qhd",
            exp_scores.astype(jnp.bfloat16),
            value_block,
            preferred_element_type=jnp.float32,
        )
        / jnp.transpose(row_total)[:, :, None]
    )
    return mixed_heads.astype(jnp.bfloat16)


def expert_partial(row_block, gate_cols, up_cols, down_rows):
    gate_out = jnp.dot(row_block, gate_cols, preferred_element_type=jnp.float32)
    up_out = jnp.dot(row_block, up_cols, preferred_element_type=jnp.float32)
    middle = (jax.nn.silu(gate_out) * up_out).astype(jnp.bfloat16)
    return jnp.dot(middle, down_rows, preferred_element_type=jnp.float32)


def by_slots(
    queries,
    key_rows,
    value_rows,
    residual,
    norm_gain,
    router_weight,
    expert_ids,
    gate_proj,
    up_proj,
    down_proj,
):
    local_tokens = residual.shape[0]
    model_width = residual.shape[1]
    latent_rows = queries.shape[0]
    head_cols = queries.shape[1]
    heads_here = head_cols // HDIM
    local_heads = head_attention(
        queries.reshape(latent_rows, heads_here, HDIM),
        key_rows.reshape(latent_rows, heads_here, HDIM),
        value_rows.reshape(latent_rows, heads_here, HDIM),
    )
    attended = lax.all_to_all(
        local_heads.reshape(latent_rows, head_cols), "seq", split_axis=0, concat_axis=1, tiled=True
    )
    hidden = (residual.astype(jnp.float32) + attended.astype(jnp.float32)).astype(jnp.bfloat16)
    hidden_f = hidden.astype(jnp.float32)
    mean_sq = jnp.mean(hidden_f * hidden_f, axis=-1, keepdims=True)
    normed = (hidden_f * lax.rsqrt(mean_sq + epsilon) * norm_gain).astype(jnp.bfloat16)
    logits = jnp.dot(normed, router_weight, preferred_element_type=jnp.float32)
    experts = router_weight.shape[1]
    capacity = 3 * local_tokens * TOP // (2 * experts)
    catalog = jnp.arange(experts, dtype=jnp.int32)
    flat_ids = expert_ids.reshape(local_tokens * TOP)
    onehot = (flat_ids[:, None] == catalog[None, :]).astype(jnp.int32)
    picked = jnp.sum(
        onehot.reshape(local_tokens, TOP, experts).astype(jnp.float32) * logits[:, None, :], axis=2
    )
    sigmoids = jax.nn.sigmoid(picked)
    gate_values = sigmoids / jnp.sum(sigmoids, axis=1, keepdims=True)
    earlier = jnp.cumsum(onehot, axis=0) - onehot
    slot_index = jnp.sum(earlier * onehot, axis=1)
    place = flat_ids * capacity + slot_index
    source_rows = jnp.repeat(normed, TOP, axis=0)
    outgoing = (
        jnp.zeros((experts * capacity, model_width), jnp.bfloat16)
        .at[place]
        .set(source_rows)
        .reshape(experts, capacity, model_width)
    )
    both_halves = lax.all_gather(
        lax.all_to_all(outgoing, "exp", split_axis=0, concat_axis=0, tiled=True),
        "seq",
        axis=0,
        tiled=True,
    )
    partial_value = expert_partial(
        both_halves.reshape(-1, model_width), gate_proj[0], up_proj[0], down_proj[0]
    ).reshape(both_halves.shape)
    summed = lax.psum_scatter(
        partial_value.astype(jnp.bfloat16), "seq", scatter_dimension=0, tiled=True
    )
    answers = lax.all_to_all(summed, "exp", split_axis=0, concat_axis=0, tiled=True)
    returned_rows = answers.reshape(experts * capacity, model_width)
    gathered = returned_rows[place].reshape(local_tokens, TOP, model_width)
    moe_sum = hidden_f
    for which_slot in range(TOP):
        moe_sum = moe_sum + gate_values[:, which_slot : which_slot + 1] * gathered[
            :, which_slot
        ].astype(jnp.float32)
    return moe_sum.astype(jnp.bfloat16)


def attention_kernel(q_ref, k_ref, v_ref, o_ref):
    for at in range(q_ref.shape[1] // HDIM):
        cols = slice(at * HDIM, (at + 1) * HDIM)
        scores = lax.dot_general(
            q_ref[:, cols],
            k_ref[:, cols],
            (((1,), (1,)), ((), ())),
            preferred_element_type=jnp.float32,
        ) * HDIM ** (-0.5)
        exp_scores = jnp.exp(scores - jnp.max(scores, axis=-1, keepdims=True))
        row_total = jnp.sum(exp_scores, axis=-1, keepdims=True)
        mixed_head = jnp.dot(
            exp_scores.astype(jnp.bfloat16), v_ref[:, cols], preferred_element_type=jnp.float32
        )
        o_ref[:, cols] = (mixed_head / row_total).astype(o_ref.dtype)


def attention(queries, key_rows, value_rows):
    rows, cols = queries.shape
    width = 2 * HDIM
    spec = pl.BlockSpec((rows, width), lambda h: (0, h))
    return pl.pallas_call(
        attention_kernel,
        grid=(cols // width,),
        in_specs=[spec] * 3,
        out_specs=spec,
        out_shape=jax.ShapeDtypeStruct((rows, cols), jnp.bfloat16),
        cost_estimate=pl.CostEstimate(
            flops=4 * rows * rows * cols,
            bytes_accessed=8 * rows * cols,
            transcendentals=rows * rows * cols // HDIM,
        ),
    )(queries, key_rows, value_rows)


def hidden_and_normed(queries, key_rows, value_rows, residual, norm_gain):
    attended = lax.all_to_all(
        attention(queries, key_rows, value_rows), "seq", split_axis=0, concat_axis=1, tiled=True
    )
    hidden = (residual.astype(jnp.float32) + attended.astype(jnp.float32)).astype(jnp.bfloat16)
    hidden_f = hidden.astype(jnp.float32)
    mean_sq = jnp.mean(hidden_f * hidden_f, axis=-1, keepdims=True)
    normed = (hidden_f * lax.rsqrt(mean_sq + epsilon) * norm_gain).astype(jnp.bfloat16)
    return hidden, normed


SHARED = 48
PIECES = 4
MESH = pl.DeviceIdType.MESH


def dense_gates(normed, ids, router_weight):
    experts = router_weight.shape[1]
    logits = jnp.dot(normed, router_weight, preferred_element_type=jnp.float32)
    catalog = jnp.arange(experts, dtype=jnp.int32)
    chosen = jnp.any(ids[:, :, None] == catalog[None, None, :], axis=1)
    sigmoids = jnp.where(chosen, jax.nn.sigmoid(logits), 0.0)
    return sigmoids / jnp.sum(sigmoids, axis=1, keepdims=True)


def expert_kernel(
    owners,
    normed_ref,
    gates_ref,
    gate_ref,
    up_ref,
    down_ref,
    out_ref,
    rows,
    sums,
    from_side,
    from_below,
    from_above,
    gate_all,
    up_all,
    down_all,
    middle,
    gates,
    local_sem,
    weight_send,
    weight_recv,
    gates_send,
    gates_recv,
    shared_send,
    shared_recv,
    side_send,
    side_recv,
    up_send,
    down_send,
    line_recv,
    back_side_send,
    back_side_recv,
    back_up_send,
    back_up_recv,
    back_down_send,
    back_down_recv,
    last_send,
    last_recv,
):
    length = owners // 2
    tokens, width = normed_ref.shape
    half = gate_ref.shape[1]
    apart = tokens - SHARED
    me = lax.axis_index("exp")
    core = lax.axis_index("seq")
    z = me // 2
    y = me % 2
    side = {"exp": me + 1 - 2 * y}
    other_core = {"seq": 1 - core}
    above = {"exp": me + 2}
    below = {"exp": me - 2}
    has_above = z + 1 < length
    has_below = z > 0

    def start_of(count):
        return pl.multiple_of(count, 16)

    line_rows = pl.ds(start_of(y * apart), tokens + SHARED)
    my_apart = pl.ds(start_of(y * (tokens + SHARED)), apart)
    side_apart = pl.ds(start_of((1 - y) * (tokens + SHARED)), apart)
    my_shared = pl.ds(start_of(apart + y * SHARED), SHARED)
    side_shared = pl.ds(start_of(apart + (1 - y) * SHARED), SHARED)
    own_rows = pl.ds(start_of(y * tokens), tokens)

    def remote(src, dst, send, recv, device):
        return pltpu.make_async_remote_copy(
            src_ref=src, dst_ref=dst, send_sem=send, recv_sem=recv, device_id=device, device_id_type=MESH
        )

    def own_weights(at):
        src = (gate_ref, up_ref, down_ref)[at]
        dst = (
            gate_all.at[:, pl.ds(0, half)],
            up_all.at[:, pl.ds(0, half)],
            down_all.at[pl.ds(0, half)],
        )[at]
        return pltpu.make_async_copy(src, dst, local_sem.at[at])

    def other_weights(at):
        src = (gate_ref, up_ref, down_ref)[at]
        dst = (
            gate_all.at[:, pl.ds(half, half)],
            up_all.at[:, pl.ds(half, half)],
            down_all.at[pl.ds(half, half)],
        )[at]
        return remote(src, dst, weight_send.at[at], weight_recv.at[at], other_core)

    def gates_copy(step):
        to = lax.rem(me + step, owners)
        return remote(
            gates_ref, gates.at[me], gates_send.at[step], gates_recv.at[step], {"exp": to}
        )

    piece_width = width // PIECES

    def columns(piece):
        return pl.ds(pl.multiple_of(piece * piece_width, 128), piece_width)

    def shared_copy(piece):
        block = rows.at[z, my_shared, columns(piece)]
        return remote(block, block, shared_send.at[piece], shared_recv.at[piece], side)

    def side_copy(at, piece):
        which = at * PIECES + piece
        block = rows.at[at, my_apart, columns(piece)]
        return remote(block, block, side_send.at[which], side_recv.at[which], side)

    def up_copy(at, piece):
        which = at * PIECES + piece
        block = rows.at[at, line_rows, columns(piece)]
        return remote(block, block, up_send.at[which], line_recv.at[which], above)

    def down_copy(at, piece):
        which = at * PIECES + piece
        block = rows.at[at, line_rows, columns(piece)]
        return remote(block, block, down_send.at[which], line_recv.at[which], below)

    def back_side_copy(at, piece):
        which = at * PIECES + piece
        return remote(
            sums.at[at, side_apart, columns(piece)],
            from_side.at[at, :, columns(piece)],
            back_side_send.at[which],
            back_side_recv.at[which],
            side,
        )

    def back_up_copy(at, piece):
        which = at * PIECES + piece
        return remote(
            sums.at[at, line_rows, columns(piece)],
            from_below.at[at, :, columns(piece)],
            back_up_send.at[which],
            back_up_recv.at[which],
            above,
        )

    def back_down_copy(at, piece):
        which = at * PIECES + piece
        return remote(
            sums.at[at, line_rows, columns(piece)],
            from_above.at[at, :, columns(piece)],
            back_down_send.at[which],
            back_down_recv.at[which],
            below,
        )

    def last_copy(piece):
        return remote(
            sums.at[z, side_shared, columns(piece)],
            from_side.at[length, pl.ds(0, SHARED), columns(piece)],
            last_send.at[piece],
            last_recv.at[piece],
            side,
        )

    barrier = pltpu.get_barrier_semaphore()
    for step in range(1, owners):
        pl.semaphore_signal(
            barrier, inc=1, device_id={"exp": lax.rem(me + step, owners)}, device_id_type=MESH
        )
    pl.semaphore_signal(barrier, inc=1, device_id=other_core, device_id_type=MESH)
    own_copy = pltpu.make_async_copy(normed_ref, rows.at[z, own_rows], local_sem.at[3])
    own_copy.start()
    own_gates = pltpu.make_async_copy(gates_ref, gates.at[me], local_sem.at[4])
    own_gates.start()
    own_copy.wait()
    pl.semaphore_wait(barrier, owners)

    for piece in range(PIECES):
        shared_copy(piece).start()
    for piece in range(PIECES):
        side_copy(z, piece).start()
    for step in range(1, owners):
        gates_copy(step).start()
    for at in range(3):
        other_weights(at).start()
    for at in range(3):
        own_weights(at).start()

    def line_start(piece, carry):
        shared_copy(piece).wait_recv()

        @pl.when(has_above)
        def _():
            up_copy(z, piece).start()

        @pl.when(has_below)
        def _():
            down_copy(z, piece).start()

        return carry

    lax.fori_loop(0, PIECES, line_start, 0)
    own_gates.wait()
    for step in range(1, owners):
        gates_copy(step).wait_recv()
    for at in range(3):
        own_weights(at).wait()
        other_weights(at).wait_recv()

    def expert_sums(at):
        grid_row = lax.broadcasted_iota(jnp.int32, (tokens, tokens), 0)
        grid_col = lax.broadcasted_iota(jnp.int32, (tokens, tokens), 1)

        def gate_column(which):
            table = gates[2 * at + which]
            mine = lax.broadcasted_iota(jnp.int32, table.shape, 0) == me
            line = jnp.sum(jnp.where(mine, table, 0.0), axis=0, keepdims=True)
            return jnp.sum(jnp.where(grid_row == grid_col, line, 0.0), axis=1, keepdims=True)

        gate_col = jnp.concatenate([gate_column(0), gate_column(1)], axis=0)

        def middle_tile(tile, carry):
            cols = pl.ds(pl.multiple_of(tile * 256, 256), 256)
            gate_out = jnp.dot(rows[at], gate_all[:, cols], preferred_element_type=jnp.float32)
            up_out = jnp.dot(rows[at], up_all[:, cols], preferred_element_type=jnp.float32)
            middle[:, cols] = (gate_out / (1.0 + jnp.exp(-gate_out)) * up_out).astype(jnp.bfloat16)
            return carry

        lax.fori_loop(0, 2 * half // 256, middle_tile, 0)

        def out_tile(tile, carry):
            cols = pl.ds(pl.multiple_of(tile * 512, 512), 512)
            part = jnp.dot(middle[...], down_all[:, cols], preferred_element_type=jnp.float32)
            sums[at, :, cols] = (part * gate_col).astype(jnp.bfloat16)
            return carry

        lax.fori_loop(0, width // 512, out_tile, 0)

    def inside(at):
        return jnp.logical_and(at >= 0, at < length)

    def gather_piece(at, piece):
        @pl.when(inside(at))
        def _():
            up_copy(at, piece).wait_recv()

            @pl.when(jnp.logical_and(at < z, has_above))
            def _():
                up_copy(at, piece).start()

            @pl.when(jnp.logical_and(at > z, has_below))
            def _():
                down_copy(at, piece).start()

            side_copy(at, piece).start()

    def compute_block(at):
        def wait_piece(piece, carry):
            side_copy(at, piece).wait_recv()
            return carry

        def send_piece(piece, carry):
            back_side_copy(at, piece).start()
            return carry

        lax.fori_loop(0, PIECES, wait_piece, 0)
        expert_sums(at)
        lax.fori_loop(0, PIECES, send_piece, 0)

    def add_rows(at, piece, first, source, count):
        def add_some(group, carry):
            into = pl.ds(start_of(first + group * 16), 16)
            what = pl.ds(start_of(group * 16), 16)
            cols = columns(piece)
            sums[at, into, cols] = (
                sums[at, into, cols].astype(jnp.float32) + source[at, what, cols].astype(jnp.float32)
            ).astype(jnp.bfloat16)
            return carry

        lax.fori_loop(0, count // 16, add_some, 0)

    def add_side(at, piece):
        back_side_copy(at, piece).wait_recv()
        add_rows(at, piece, y * (tokens + SHARED), from_side, apart)

    def add_below(at, piece):
        back_up_copy(at, piece).wait_recv()
        add_rows(at, piece, y * apart, from_below, tokens + SHARED)

    def add_above(at, piece):
        back_down_copy(at, piece).wait_recv()
        add_rows(at, piece, y * apart, from_above, tokens + SHARED)

    def return_up(at, piece, here):
        @pl.when(jnp.logical_and(here, jnp.logical_and(at > z, inside(at))))
        def _():
            add_side(at, piece)

            @pl.when(has_below)
            def _():
                add_below(at, piece)

            back_up_copy(at, piece).start()

    def return_down(at, piece, here):
        @pl.when(jnp.logical_and(here, jnp.logical_and(at < z, inside(at))))
        def _():
            add_side(at, piece)

            @pl.when(has_above)
            def _():
                add_above(at, piece)

            back_down_copy(at, piece).start()

    low_half = z < length // 2

    def one_round(away, carry):
        @pl.when(away < length)
        def _():
            def both_pieces(piece, inner):
                gather_piece(z - away, piece)
                gather_piece(z + away, piece)
                return inner

            lax.fori_loop(0, PIECES, both_pieces, 0)

        def near_block(which, inner):
            at = jnp.where(which == 0, z - away + 1, z + away - 1)

            @pl.when(jnp.logical_and(inside(at), jnp.logical_or(which == 0, away > 1)))
            def _():
                compute_block(at)

            return inner

        lax.fori_loop(0, 2, near_block, 0)

        def return_piece(piece, inner):
            far = away - 2
            return_up(far, piece, low_half)
            return_down(length - 1 - far, piece, True)
            return_up(far, piece, jnp.logical_not(low_half))
            return inner

        @pl.when(away > 2)
        def _():
            lax.fori_loop(0, PIECES, return_piece, 0)

        return carry

    lax.fori_loop(1, length + 2, one_round, 0)

    def finish_piece(piece, carry):
        add_side(z, piece)

        @pl.when(has_below)
        def _():
            add_below(z, piece)

        @pl.when(has_above)
        def _():
            add_above(z, piece)

        last_copy(piece).start()
        out_ref[:, columns(piece)] = sums[z, own_rows, columns(piece)]
        return carry

    lax.fori_loop(0, PIECES, finish_piece, 0)
    out_shared = pl.ds(start_of((1 - y) * apart), SHARED)

    def last_piece(piece, carry):
        last_copy(piece).wait_recv()
        cols = columns(piece)
        out_ref[out_shared, cols] = (
            out_ref[out_shared, cols].astype(jnp.float32)
            + from_side[length, pl.ds(0, SHARED), cols].astype(jnp.float32)
        ).astype(jnp.bfloat16)
        return carry

    lax.fori_loop(0, PIECES, last_piece, 0)
    for piece in range(PIECES):
        last_copy(piece).wait_send()
        shared_copy(piece).wait_send()
    for step in range(1, owners):
        gates_copy(step).wait_send()
    for at in range(3):
        other_weights(at).wait_send()

    def drain(which, carry):
        at = which // PIECES
        piece = which % PIECES
        side_copy(at, piece).wait_send()
        back_side_copy(at, piece).wait_send()

        @pl.when(jnp.logical_and(at <= z, has_above))
        def _():
            up_copy(at, piece).wait_send()

        @pl.when(jnp.logical_and(at >= z, has_below))
        def _():
            down_copy(at, piece).wait_send()

        @pl.when(at > z)
        def _():
            back_up_copy(at, piece).wait_send()

        @pl.when(at < z)
        def _():
            back_down_copy(at, piece).wait_send()

        return carry

    lax.fori_loop(0, length * PIECES, drain, 0)


def routed_experts(normed, gates, gate_half, up_half, down_half):
    tokens, width = normed.shape
    owners = gates.shape[0]
    length = owners // 2
    half = gate_half.shape[1]
    anywhere = pl.BlockSpec(memory_space=pl.ANY)
    dma = pltpu.SemaphoreType.DMA
    return pl.pallas_call(
        functools.partial(expert_kernel, owners),
        in_specs=[anywhere] * 5,
        out_specs=pl.BlockSpec(memory_space=pltpu.VMEM),
        out_shape=jax.ShapeDtypeStruct((tokens, width), jnp.bfloat16),
        scratch_shapes=[
            pltpu.VMEM((length, 2 * tokens, width), jnp.bfloat16),
            pltpu.VMEM((length, 2 * tokens, width), jnp.bfloat16),
            pltpu.VMEM((length + 1, tokens - SHARED, width), jnp.bfloat16),
            pltpu.VMEM((length, tokens + SHARED, width), jnp.bfloat16),
            pltpu.VMEM((length, tokens + SHARED, width), jnp.bfloat16),
            pltpu.VMEM((width, 2 * half), jnp.bfloat16),
            pltpu.VMEM((width, 2 * half), jnp.bfloat16),
            pltpu.VMEM((2 * half, width), jnp.bfloat16),
            pltpu.VMEM((2 * tokens, 2 * half), jnp.bfloat16),
            pltpu.VMEM((owners, owners, tokens), jnp.float32),
            dma((5,)),
            dma((3,)),
            dma((3,)),
            dma((owners,)),
            dma((owners,)),
            dma((PIECES,)),
            dma((PIECES,)),
        ]
        + [dma((length * PIECES,))] * 11
        + [dma((PIECES,))] * 2,
        compiler_params=pltpu.CompilerParams(
            collective_id=0, has_side_effects=True, vmem_limit_bytes=58 * 1024 * 1024
        ),
        cost_estimate=pl.CostEstimate(
            flops=12 * owners * tokens * width * half,
            bytes_accessed=12 * width * half,
            transcendentals=2 * owners * tokens * half,
        ),
    )(normed, gates, gate_half, up_half, down_half)


def by_rows(
    queries,
    key_rows,
    value_rows,
    residual,
    norm_gain,
    router_weight,
    expert_ids,
    gate_proj,
    up_proj,
    down_proj,
):
    hidden, normed = hidden_and_normed(queries, key_rows, value_rows, residual, norm_gain)
    gates = jnp.transpose(dense_gates(normed, expert_ids, router_weight))
    summed = routed_experts(normed, gates, gate_proj[0], up_proj[0], down_proj[0])
    return (hidden.astype(jnp.float32) + summed.astype(jnp.float32)).astype(jnp.bfloat16)


def solution(mesh):
    return jax.shard_map(
        by_rows if mesh.shape["exp"] == 8 else by_slots,
        mesh=mesh,
        in_specs=(
            P(("groups", "exp"), "seq"),
            P(("groups", "exp"), "seq"),
            P(("groups", "exp"), "seq"),
            P(("groups", "exp", "seq"), None),
            P(),
            P(),
            P(("groups", "exp", "seq"), None),
            P("exp", None, "seq"),
            P("exp", None, "seq"),
            P("exp", "seq", None),
        ),
        out_specs=P(("groups", "exp", "seq"), None),
        check_vma=False,
    )
```

```python
import functools

import jax
import jax.numpy as jnp
from jax import lax
from jax.experimental import pallas as pl
from jax.experimental.pallas import tpu as pltpu
from jax.sharding import PartitionSpec as P

HDIM = 128
TOP = 4


epsilon = 1e-06


def head_attention(query_block, key_block, value_block):
    scores = jnp.einsum(
        "qhd,khd->hqk", query_block, key_block, preferred_element_type=jnp.float32
    ) * HDIM ** (-0.5)
    row_top = jnp.max(scores, axis=-1, keepdims=True)
    exp_scores = jnp.exp(scores - row_top)
    row_total = jnp.sum(exp_scores, axis=-1)
    mixed_heads = (
        jnp.einsum(
            "hqk,khd->qhd",
            exp_scores.astype(jnp.bfloat16),
            value_block,
            preferred_element_type=jnp.float32,
        )
        / jnp.transpose(row_total)[:, :, None]
    )
    return mixed_heads.astype(jnp.bfloat16)


def expert_partial(row_block, gate_cols, up_cols, down_rows):
    gate_out = jnp.dot(row_block, gate_cols, preferred_element_type=jnp.float32)
    up_out = jnp.dot(row_block, up_cols, preferred_element_type=jnp.float32)
    middle = (jax.nn.silu(gate_out) * up_out).astype(jnp.bfloat16)
    return jnp.dot(middle, down_rows, preferred_element_type=jnp.float32)


def by_slots(
    queries,
    key_rows,
    value_rows,
    residual,
    norm_gain,
    router_weight,
    expert_ids,
    gate_proj,
    up_proj,
    down_proj,
):
    local_tokens = residual.shape[0]
    model_width = residual.shape[1]
    latent_rows = queries.shape[0]
    head_cols = queries.shape[1]
    heads_here = head_cols // HDIM
    local_heads = head_attention(
        queries.reshape(latent_rows, heads_here, HDIM),
        key_rows.reshape(latent_rows, heads_here, HDIM),
        value_rows.reshape(latent_rows, heads_here, HDIM),
    )
    attended = lax.all_to_all(
        local_heads.reshape(latent_rows, head_cols), "seq", split_axis=0, concat_axis=1, tiled=True
    )
    hidden = (residual.astype(jnp.float32) + attended.astype(jnp.float32)).astype(jnp.bfloat16)
    hidden_f = hidden.astype(jnp.float32)
    mean_sq = jnp.mean(hidden_f * hidden_f, axis=-1, keepdims=True)
    normed = (hidden_f * lax.rsqrt(mean_sq + epsilon) * norm_gain).astype(jnp.bfloat16)
    logits = jnp.dot(normed, router_weight, preferred_element_type=jnp.float32)
    experts = router_weight.shape[1]
    capacity = 3 * local_tokens * TOP // (2 * experts)
    catalog = jnp.arange(experts, dtype=jnp.int32)
    flat_ids = expert_ids.reshape(local_tokens * TOP)
    onehot = (flat_ids[:, None] == catalog[None, :]).astype(jnp.int32)
    picked = jnp.sum(
        onehot.reshape(local_tokens, TOP, experts).astype(jnp.float32) * logits[:, None, :], axis=2
    )
    sigmoids = jax.nn.sigmoid(picked)
    gate_values = sigmoids / jnp.sum(sigmoids, axis=1, keepdims=True)
    earlier = jnp.cumsum(onehot, axis=0) - onehot
    slot_index = jnp.sum(earlier * onehot, axis=1)
    place = flat_ids * capacity + slot_index
    source_rows = jnp.repeat(normed, TOP, axis=0)
    outgoing = (
        jnp.zeros((experts * capacity, model_width), jnp.bfloat16)
        .at[place]
        .set(source_rows)
        .reshape(experts, capacity, model_width)
    )
    both_halves = lax.all_gather(
        lax.all_to_all(outgoing, "exp", split_axis=0, concat_axis=0, tiled=True),
        "seq",
        axis=0,
        tiled=True,
    )
    partial_value = expert_partial(
        both_halves.reshape(-1, model_width), gate_proj[0], up_proj[0], down_proj[0]
    ).reshape(both_halves.shape)
    summed = lax.psum_scatter(
        partial_value.astype(jnp.bfloat16), "seq", scatter_dimension=0, tiled=True
    )
    answers = lax.all_to_all(summed, "exp", split_axis=0, concat_axis=0, tiled=True)
    returned_rows = answers.reshape(experts * capacity, model_width)
    gathered = returned_rows[place].reshape(local_tokens, TOP, model_width)
    moe_sum = hidden_f
    for which_slot in range(TOP):
        moe_sum = moe_sum + gate_values[:, which_slot : which_slot + 1] * gathered[
            :, which_slot
        ].astype(jnp.float32)
    return moe_sum.astype(jnp.bfloat16)


def attention_kernel(q_ref, k_ref, v_ref, o_ref):
    for at in range(q_ref.shape[1] // HDIM):
        cols = slice(at * HDIM, (at + 1) * HDIM)
        scores = lax.dot_general(
            q_ref[:, cols],
            k_ref[:, cols],
            (((1,), (1,)), ((), ())),
            preferred_element_type=jnp.float32,
        ) * HDIM ** (-0.5)
        exp_scores = jnp.exp(scores - jnp.max(scores, axis=-1, keepdims=True))
        row_total = jnp.sum(exp_scores, axis=-1, keepdims=True)
        mixed_head = jnp.dot(
            exp_scores.astype(jnp.bfloat16), v_ref[:, cols], preferred_element_type=jnp.float32
        )
        o_ref[:, cols] = (mixed_head / row_total).astype(o_ref.dtype)


def attention(queries, key_rows, value_rows):
    rows, cols = queries.shape
    width = 2 * HDIM
    spec = pl.BlockSpec((rows, width), lambda h: (0, h))
    return pl.pallas_call(
        attention_kernel,
        grid=(cols // width,),
        in_specs=[spec] * 3,
        out_specs=spec,
        out_shape=jax.ShapeDtypeStruct((rows, cols), jnp.bfloat16),
        cost_estimate=pl.CostEstimate(
            flops=4 * rows * rows * cols,
            bytes_accessed=8 * rows * cols,
            transcendentals=rows * rows * cols // HDIM,
        ),
    )(queries, key_rows, value_rows)


def hidden_and_normed(queries, key_rows, value_rows, residual, norm_gain):
    attended = lax.all_to_all(
        attention(queries, key_rows, value_rows), "seq", split_axis=0, concat_axis=1, tiled=True
    )
    hidden = (residual.astype(jnp.float32) + attended.astype(jnp.float32)).astype(jnp.bfloat16)
    hidden_f = hidden.astype(jnp.float32)
    mean_sq = jnp.mean(hidden_f * hidden_f, axis=-1, keepdims=True)
    normed = (hidden_f * lax.rsqrt(mean_sq + epsilon) * norm_gain).astype(jnp.bfloat16)
    return hidden, normed


SHARED = 48
PIECES = 4
MESH = pl.DeviceIdType.MESH


def dense_gates(normed, ids, router_weight):
    experts = router_weight.shape[1]
    logits = jnp.dot(normed, router_weight, preferred_element_type=jnp.float32)
    catalog = jnp.arange(experts, dtype=jnp.int32)
    chosen = jnp.any(ids[:, :, None] == catalog[None, None, :], axis=1)
    sigmoids = jnp.where(chosen, jax.nn.sigmoid(logits), 0.0)
    return sigmoids / jnp.sum(sigmoids, axis=1, keepdims=True)


def expert_kernel(
    owners,
    normed_ref,
    gates_ref,
    gate_ref,
    up_ref,
    down_ref,
    out_ref,
    rows,
    sums,
    from_side,
    from_below,
    from_above,
    gate_all,
    up_all,
    down_all,
    middle,
    gates,
    local_sem,
    weight_send,
    weight_recv,
    gates_send,
    gates_recv,
    shared_send,
    shared_recv,
    side_send,
    side_recv,
    up_send,
    down_send,
    line_recv,
    back_side_send,
    back_side_recv,
    back_up_send,
    back_up_recv,
    back_down_send,
    back_down_recv,
    last_send,
    last_recv,
):
    length = owners // 2
    tokens, width = normed_ref.shape
    half = gate_ref.shape[1]
    apart = tokens - SHARED
    me = lax.axis_index("exp")
    core = lax.axis_index("seq")
    z = me // 2
    y = me % 2
    side = {"exp": me + 1 - 2 * y}
    other_core = {"seq": 1 - core}
    above = {"exp": me + 2}
    below = {"exp": me - 2}
    has_above = z + 1 < length
    has_below = z > 0

    def start_of(count):
        return pl.multiple_of(count, 16)

    line_rows = pl.ds(start_of(y * apart), tokens + SHARED)
    my_apart = pl.ds(start_of(y * (tokens + SHARED)), apart)
    side_apart = pl.ds(start_of((1 - y) * (tokens + SHARED)), apart)
    my_shared = pl.ds(start_of(apart + y * SHARED), SHARED)
    side_shared = pl.ds(start_of(apart + (1 - y) * SHARED), SHARED)
    own_rows = pl.ds(start_of(y * tokens), tokens)

    def remote(src, dst, send, recv, device):
        return pltpu.make_async_remote_copy(
            src_ref=src, dst_ref=dst, send_sem=send, recv_sem=recv, device_id=device, device_id_type=MESH
        )

    def own_weights(at):
        src = (gate_ref, up_ref, down_ref)[at]
        dst = (
            gate_all.at[:, pl.ds(0, half)],
            up_all.at[:, pl.ds(0, half)],
            down_all.at[pl.ds(0, half)],
        )[at]
        return pltpu.make_async_copy(src, dst, local_sem.at[at])

    def other_weights(at):
        src = (gate_ref, up_ref, down_ref)[at]
        dst = (
            gate_all.at[:, pl.ds(half, half)],
            up_all.at[:, pl.ds(half, half)],
            down_all.at[pl.ds(half, half)],
        )[at]
        return remote(src, dst, weight_send.at[at], weight_recv.at[at], other_core)

    def gates_copy(step):
        to = lax.rem(me + step, owners)
        return remote(
            gates_ref, gates.at[me], gates_send.at[step], gates_recv.at[step], {"exp": to}
        )

    piece_width = width // PIECES

    def columns(piece):
        return pl.ds(pl.multiple_of(piece * piece_width, 128), piece_width)

    def shared_copy(piece):
        block = rows.at[z, my_shared, columns(piece)]
        return remote(block, block, shared_send.at[piece], shared_recv.at[piece], side)

    def side_copy(at, piece):
        which = at * PIECES + piece
        block = rows.at[at, my_apart, columns(piece)]
        return remote(block, block, side_send.at[which], side_recv.at[which], side)

    def up_copy(at, piece):
        which = at * PIECES + piece
        block = rows.at[at, line_rows, columns(piece)]
        return remote(block, block, up_send.at[which], line_recv.at[which], above)

    def down_copy(at, piece):
        which = at * PIECES + piece
        block = rows.at[at, line_rows, columns(piece)]
        return remote(block, block, down_send.at[which], line_recv.at[which], below)

    def back_side_copy(at, piece):
        which = at * PIECES + piece
        return remote(
            sums.at[at, side_apart, columns(piece)],
            from_side.at[at, :, columns(piece)],
            back_side_send.at[which],
            back_side_recv.at[which],
            side,
        )

    def back_up_copy(at, piece):
        which = at * PIECES + piece
        return remote(
            sums.at[at, line_rows, columns(piece)],
            from_below.at[at, :, columns(piece)],
            back_up_send.at[which],
            back_up_recv.at[which],
            above,
        )

    def back_down_copy(at, piece):
        which = at * PIECES + piece
        return remote(
            sums.at[at, line_rows, columns(piece)],
            from_above.at[at, :, columns(piece)],
            back_down_send.at[which],
            back_down_recv.at[which],
            below,
        )

    def last_copy(piece):
        return remote(
            sums.at[z, side_shared, columns(piece)],
            from_side.at[length, pl.ds(0, SHARED), columns(piece)],
            last_send.at[piece],
            last_recv.at[piece],
            side,
        )

    barrier = pltpu.get_barrier_semaphore()
    for step in range(1, owners):
        pl.semaphore_signal(
            barrier, inc=1, device_id={"exp": lax.rem(me + step, owners)}, device_id_type=MESH
        )
    pl.semaphore_signal(barrier, inc=1, device_id=other_core, device_id_type=MESH)
    own_copy = pltpu.make_async_copy(normed_ref, rows.at[z, own_rows], local_sem.at[3])
    own_copy.start()
    own_gates = pltpu.make_async_copy(gates_ref, gates.at[me], local_sem.at[4])
    own_gates.start()
    own_copy.wait()
    pl.semaphore_wait(barrier, owners)

    for piece in range(PIECES):
        shared_copy(piece).start()
    for piece in range(PIECES):
        side_copy(z, piece).start()
    for step in range(1, owners):
        gates_copy(step).start()
    for at in range(3):
        other_weights(at).start()
    for at in range(3):
        own_weights(at).start()

    def line_start(piece, carry):
        shared_copy(piece).wait_recv()

        @pl.when(has_above)
        def _():
            up_copy(z, piece).start()

        @pl.when(has_below)
        def _():
            down_copy(z, piece).start()

        return carry

    lax.fori_loop(0, PIECES, line_start, 0)
    own_gates.wait()
    for step in range(1, owners):
        gates_copy(step).wait_recv()
    for at in range(3):
        own_weights(at).wait()
        other_weights(at).wait_recv()

    def expert_sums(at):
        grid_row = lax.broadcasted_iota(jnp.int32, (tokens, tokens), 0)
        grid_col = lax.broadcasted_iota(jnp.int32, (tokens, tokens), 1)

        def gate_column(which):
            table = gates[2 * at + which]
            mine = lax.broadcasted_iota(jnp.int32, table.shape, 0) == me
            line = jnp.sum(jnp.where(mine, table, 0.0), axis=0, keepdims=True)
            return jnp.sum(jnp.where(grid_row == grid_col, line, 0.0), axis=1, keepdims=True)

        gate_col = jnp.concatenate([gate_column(0), gate_column(1)], axis=0)

        def middle_tile(tile, carry):
            cols = pl.ds(pl.multiple_of(tile * 256, 256), 256)
            gate_out = jnp.dot(rows[at], gate_all[:, cols], preferred_element_type=jnp.float32)
            up_out = jnp.dot(rows[at], up_all[:, cols], preferred_element_type=jnp.float32)
            middle[:, cols] = (gate_out / (1.0 + jnp.exp(-gate_out)) * up_out).astype(jnp.bfloat16)
            return carry

        lax.fori_loop(0, 2 * half // 256, middle_tile, 0)

        def out_tile(tile, carry):
            cols = pl.ds(pl.multiple_of(tile * 512, 512), 512)
            part = jnp.dot(middle[...], down_all[:, cols], preferred_element_type=jnp.float32)
            sums[at, :, cols] = (part * gate_col).astype(jnp.bfloat16)
            return carry

        lax.fori_loop(0, width // 512, out_tile, 0)

    def inside(at):
        return jnp.logical_and(at >= 0, at < length)

    def gather_piece(at, piece):
        @pl.when(inside(at))
        def _():
            up_copy(at, piece).wait_recv()

            @pl.when(jnp.logical_and(at < z, has_above))
            def _():
                up_copy(at, piece).start()

            @pl.when(jnp.logical_and(at > z, has_below))
            def _():
                down_copy(at, piece).start()

            side_copy(at, piece).start()

    def compute_block(at):
        def wait_piece(piece, carry):
            side_copy(at, piece).wait_recv()
            return carry

        def send_piece(piece, carry):
            back_side_copy(at, piece).start()
            return carry

        lax.fori_loop(0, PIECES, wait_piece, 0)
        expert_sums(at)
        lax.fori_loop(0, PIECES, send_piece, 0)

    def add_rows(at, piece, first, source, count):
        def add_some(group, carry):
            into = pl.ds(start_of(first + group * 16), 16)
            what = pl.ds(start_of(group * 16), 16)
            cols = columns(piece)
            sums[at, into, cols] = (
                sums[at, into, cols].astype(jnp.float32) + source[at, what, cols].astype(jnp.float32)
            ).astype(jnp.bfloat16)
            return carry

        lax.fori_loop(0, count // 16, add_some, 0)

    def add_side(at, piece):
        back_side_copy(at, piece).wait_recv()
        add_rows(at, piece, y * (tokens + SHARED), from_side, apart)

    def add_below(at, piece):
        back_up_copy(at, piece).wait_recv()
        add_rows(at, piece, y * apart, from_below, tokens + SHARED)

    def add_above(at, piece):
        back_down_copy(at, piece).wait_recv()
        add_rows(at, piece, y * apart, from_above, tokens + SHARED)

    def return_up(at, piece, here):
        @pl.when(jnp.logical_and(here, jnp.logical_and(at > z, inside(at))))
        def _():
            add_side(at, piece)

            @pl.when(has_below)
            def _():
                add_below(at, piece)

            back_up_copy(at, piece).start()

    def return_down(at, piece, here):
        @pl.when(jnp.logical_and(here, jnp.logical_and(at < z, inside(at))))
        def _():
            add_side(at, piece)

            @pl.when(has_above)
            def _():
                add_above(at, piece)

            back_down_copy(at, piece).start()

    low_half = z < length // 2

    def one_round(away, carry):
        def both_pieces(piece, inner):
            far = away - 2

            @pl.when(far > 0)
            def _():
                return_up(far, piece, low_half)
                return_down(length - 1 - far, piece, True)
                return_up(far, piece, jnp.logical_not(low_half))

            @pl.when(away < length)
            def _():
                gather_piece(z - away, piece)
                gather_piece(z + away, piece)

            return inner

        lax.fori_loop(0, PIECES, both_pieces, 0)

        def near_block(which, inner):
            at = jnp.where(which == 0, z - away + 1, z + away - 1)

            @pl.when(jnp.logical_and(inside(at), jnp.logical_or(which == 0, away > 1)))
            def _():
                compute_block(at)

            return inner

        lax.fori_loop(0, 2, near_block, 0)

        return carry

    lax.fori_loop(1, length + 2, one_round, 0)

    def finish_piece(piece, carry):
        add_side(z, piece)

        @pl.when(has_below)
        def _():
            add_below(z, piece)

        @pl.when(has_above)
        def _():
            add_above(z, piece)

        last_copy(piece).start()
        out_ref[:, columns(piece)] = sums[z, own_rows, columns(piece)]
        return carry

    lax.fori_loop(0, PIECES, finish_piece, 0)
    out_shared = pl.ds(start_of((1 - y) * apart), SHARED)

    def last_piece(piece, carry):
        last_copy(piece).wait_recv()
        cols = columns(piece)
        out_ref[out_shared, cols] = (
            out_ref[out_shared, cols].astype(jnp.float32)
            + from_side[length, pl.ds(0, SHARED), cols].astype(jnp.float32)
        ).astype(jnp.bfloat16)
        return carry

    lax.fori_loop(0, PIECES, last_piece, 0)
    for piece in range(PIECES):
        last_copy(piece).wait_send()
        shared_copy(piece).wait_send()
    for step in range(1, owners):
        gates_copy(step).wait_send()
    for at in range(3):
        other_weights(at).wait_send()

    def drain(which, carry):
        at = which // PIECES
        piece = which % PIECES
        side_copy(at, piece).wait_send()
        back_side_copy(at, piece).wait_send()

        @pl.when(jnp.logical_and(at <= z, has_above))
        def _():
            up_copy(at, piece).wait_send()

        @pl.when(jnp.logical_and(at >= z, has_below))
        def _():
            down_copy(at, piece).wait_send()

        @pl.when(at > z)
        def _():
            back_up_copy(at, piece).wait_send()

        @pl.when(at < z)
        def _():
            back_down_copy(at, piece).wait_send()

        return carry

    lax.fori_loop(0, length * PIECES, drain, 0)


def routed_experts(normed, gates, gate_half, up_half, down_half):
    tokens, width = normed.shape
    owners = gates.shape[0]
    length = owners // 2
    half = gate_half.shape[1]
    anywhere = pl.BlockSpec(memory_space=pl.ANY)
    dma = pltpu.SemaphoreType.DMA
    return pl.pallas_call(
        functools.partial(expert_kernel, owners),
        in_specs=[anywhere] * 5,
        out_specs=pl.BlockSpec(memory_space=pltpu.VMEM),
        out_shape=jax.ShapeDtypeStruct((tokens, width), jnp.bfloat16),
        scratch_shapes=[
            pltpu.VMEM((length, 2 * tokens, width), jnp.bfloat16),
            pltpu.VMEM((length, 2 * tokens, width), jnp.bfloat16),
            pltpu.VMEM((length + 1, tokens - SHARED, width), jnp.bfloat16),
            pltpu.VMEM((length, tokens + SHARED, width), jnp.bfloat16),
            pltpu.VMEM((length, tokens + SHARED, width), jnp.bfloat16),
            pltpu.VMEM((width, 2 * half), jnp.bfloat16),
            pltpu.VMEM((width, 2 * half), jnp.bfloat16),
            pltpu.VMEM((2 * half, width), jnp.bfloat16),
            pltpu.VMEM((2 * tokens, 2 * half), jnp.bfloat16),
            pltpu.VMEM((owners, owners, tokens), jnp.float32),
            dma((5,)),
            dma((3,)),
            dma((3,)),
            dma((owners,)),
            dma((owners,)),
            dma((PIECES,)),
            dma((PIECES,)),
        ]
        + [dma((length * PIECES,))] * 11
        + [dma((PIECES,))] * 2,
        compiler_params=pltpu.CompilerParams(
            collective_id=0, has_side_effects=True, vmem_limit_bytes=58 * 1024 * 1024
        ),
        cost_estimate=pl.CostEstimate(
            flops=12 * owners * tokens * width * half,
            bytes_accessed=12 * width * half,
            transcendentals=2 * owners * tokens * half,
        ),
    )(normed, gates, gate_half, up_half, down_half)


def by_rows(
    queries,
    key_rows,
    value_rows,
    residual,
    norm_gain,
    router_weight,
    expert_ids,
    gate_proj,
    up_proj,
    down_proj,
):
    hidden, normed = hidden_and_normed(queries, key_rows, value_rows, residual, norm_gain)
    gates = jnp.transpose(dense_gates(normed, expert_ids, router_weight))
    summed = routed_experts(normed, gates, gate_proj[0], up_proj[0], down_proj[0])
    return (hidden.astype(jnp.float32) + summed.astype(jnp.float32)).astype(jnp.bfloat16)


def solution(mesh):
    return jax.shard_map(
        by_rows if mesh.shape["exp"] == 8 else by_slots,
        mesh=mesh,
        in_specs=(
            P(("groups", "exp"), "seq"),
            P(("groups", "exp"), "seq"),
            P(("groups", "exp"), "seq"),
            P(("groups", "exp", "seq"), None),
            P(),
            P(),
            P(("groups", "exp", "seq"), None),
            P("exp", None, "seq"),
            P("exp", None, "seq"),
            P("exp", "seq", None),
        ),
        out_specs=P(("groups", "exp", "seq"), None),
        check_vma=False,
    )
```
